32 devices in a mesh: groups: 1, tm: 8 (over z, y), expert: 2 (over x), head: 2 (over core).
Axes of the slice: x: 2, y: 2, z: 4, core: 2. Of those that a mesh axis runs over, the one named last changes fastest.
Arguments:
- queries: bfloat16 [2, 1024, 2048], P(('groups', 'expert'), 'tm', 'head'), may hold values from -40 to 40
- keys: bfloat16 [2, 1024, 256], P(('groups', 'expert'), 'tm', 'head'), may hold values from -4.5 to 4.5
- values: bfloat16 [2, 1024, 256], P(('groups', 'expert'), 'tm', 'head'), may hold values from -12 to 12
- segments: int32 [2, 1024], P(('groups', 'expert')), may hold values from 0 to 31, never falling along the last dimension, each value on 1 to 128 neighbouring positions
- resid: bfloat16 [2, 1024, 2048], P(('groups', 'expert'), 'tm', 'head'), may hold values from -6 to 6
- output_weight: bfloat16 [2048, 2048], P('head', 'expert'), may hold values from -0.375 to 0.375
- norm_gain: float32 [2048], P('head'), may hold values from 0.5 to 1.5
- routes: int32 [2, 1024, 8], P(('groups', 'expert'), 'tm'), may hold values from 0 to 15, all different within a row; in each aligned block of 128 rows (0 to 127, 128 to 255, ..., all dimensions but the last counted through in order) at most 96 rows name the same one
- route_weights: float32 [2, 1024, 8], P(('groups', 'expert'), 'tm'), may hold values from 0.05 to 0.3
- w_gu: bfloat16 [16, 2048, 768], P(('tm', 'expert'), 'head'), may hold values from -0.125 to 0.125
- w_down: bfloat16 [16, 384, 2048], P(('tm', 'expert'), None, 'head'), may hold values from -0.3125 to 0.3125
Outputs:
- layer_out: bfloat16 [2, 1024, 2048], P(('groups', 'expert'), 'tm', 'head')
The draws below stay inside these ranges and needn't reach their ends.
Inputs may be any that keep to these rules, and one draw needn't show every extreme that they name: `routes`: each row names 8 different experts; among the 128 positions of one device's aligned block no expert is named more than 96 times, a bound that some block reaches. `segments`: segment numbers never fall along a sequence; every segment holds 1 to 128 positions.
All inputs are finite; a program needn't handle non-finite values.
Results may differ from the reference program's by a relative error of at most 0.012.
Values may be sent and summed in bfloat16 or wider, within the bound.
A program may use at most 64 MiB of HBM per device.

```python
import math
import jax
import jax.numpy as jnp
import numpy as np
from jax import lax

D = 2048
QH = 16
KVH = 2
HD = 128
FF = 384
TOP = 8
TOK_DEV = 128
SEQ = 1024
NSEQ = 2
EXPERTS = 16
CAP = 96
N_TM = 8
N_EXPERT = 2
N_HEAD = 2


def draw_queries(key, part):
    key = jax.random.fold_in(key, 3)
    shape = (NSEQ, SEQ, QH * HD)
    base = jnp.clip(1.5 * jax.random.normal(key, shape, jnp.float32), -9.0, 9.0)
    return base.astype(jnp.bfloat16)


def draw_keys(key, part):
    key = jax.random.fold_in(key, 5)
    shape = (NSEQ, SEQ, KVH * HD)
    base = jnp.clip(jax.random.normal(key, shape, jnp.float32), -4.5, 4.5)
    return base.astype(jnp.bfloat16)


def levels(rng, dims, shards, low, high):
    factor_of, own = 1.0, jax.random.fold_in(rng, 6)
    for dim, shards_of in shards:
        heights = jnp.exp(jax.random.uniform(jax.random.fold_in(own, dim), (shards_of,), jnp.float32, low / len(shards), high / len(shards)))
        factor_of = factor_of * jnp.repeat(heights, dims[dim] // shards_of).reshape([-1 if axis == dim else 1 for axis in range(len(dims))])
    return factor_of


def split_up(count, total, most, skew):
    portions = [(1 << 20) // math.isqrt(grade ** skew) + 1 for grade in range(2, count + 1)]
    surplus, counts = total - most - (count - 1), [1] * (count - 1)
    while surplus > 0:
        candidates = [i for i in range(count - 1) if counts[i] < most]
        pool, left = sum([portions[i] for i in candidates]), surplus
        for i in candidates:
            more = min(most - counts[i], max(1, left * portions[i] // pool), surplus)
            counts[i] = counts[i] + more
            surplus = surplus - more
    return np.array([most] + counts)


def ragged(stream_key, number_of, total, bound, slope):
    if number_of == 2:
        one = jax.random.randint(stream_key, (), max(1, total - bound), min(bound, total - 1) + 1)
        return jnp.stack([one, total - one])
    tallies = jnp.asarray(split_up(number_of, total, bound, slope), jnp.int32)
    couples = (number_of - 1) // 2
    donor, taker = tallies[1:1 + 2 * couples:2], tallies[2:2 + 2 * couples:2]
    margin = jnp.minimum(donor - 1, bound - taker)
    shifted = jax.random.randint(jax.random.fold_in(stream_key, 1), (couples,), 0, 1 << 20) % (margin + 1)
    tallies = tallies.at[1:1 + 2 * couples:2].set(donor - shifted).at[2:2 + 2 * couples:2].set(taker + shifted)
    return tallies[jax.random.permutation(jax.random.fold_in(stream_key, 2), number_of)]


def assign_block(key, own, number, rows, amount, top, reach, skew):
    order = jax.random.permutation(key, amount)
    crowded, common = portions_of(amount, rows * top, reach, skew, True), portions_of(amount, rows * top, reach, skew, False)
    places = jnp.arange(amount)

    def named(tallies, rotation):
        used = int((tallies > 0).sum())
        fixed = max(1, used // 4)
        moved = fixed + (places - fixed + rotation * (used - fixed)) % max(1, amount - fixed)
        return jnp.zeros((amount,), jnp.int32).at[order[jnp.where(places < fixed, places, moved)]].set(jnp.asarray(tallies, jnp.int32))

    tallies = jnp.where(number % 4 == 0, named(crowded, number // 4), named(common, number - number // 4 - 1))
    mixed = jax.random.permutation(jax.random.fold_in(own, 3), amount)
    donor, sink = mixed[0:amount // 2 * 2:2], mixed[1:amount // 2 * 2:2]
    room = jnp.minimum(tallies[donor] - 1, reach - tallies[sink]) // 2
    room = jnp.where((donor == order[0]) | (sink == order[0]) | (tallies[sink] == 0), 0, jnp.maximum(room, 0))
    moved = jax.random.randint(jax.random.fold_in(own, 4), (amount // 2,), 0, 1 << 20) % (room + 1)
    tallies = tallies.at[donor].add(-moved).at[sink].add(moved)
    items = jnp.searchsorted(jnp.cumsum(tallies), jnp.arange(rows * top), side="right").astype(jnp.int32)
    grid = items.reshape(top, rows).T
    grid = grid[jax.random.permutation(jax.random.fold_in(own, 1), rows)]
    rotation = jax.random.randint(jax.random.fold_in(own, 2), (rows, 1), 0, top)
    return jnp.take_along_axis(grid, (jnp.arange(top)[None, :] + rotation) % top, axis=1)


def portions_of(amount, total, reach, lean, full):
    portions = [(1 << 20) // math.isqrt(grade ** lean) + 1 for grade in range(1, amount + 1)]
    largest = reach if full else min(reach, max(-(-total // amount), total * portions[0] // sum(portions)))
    least = 1 if total - largest >= amount - 1 else 0
    holding, spare = [largest] + [least] * (amount - 1), total - largest - least * (amount - 1)
    while spare > 0:
        movable = [i for i in range(1, amount) if holding[i] < largest] or [i for i in range(1, amount) if holding[i] < reach]
        whole, budget = sum([portions[i] for i in movable]), spare
        for i in movable:
            extra = min(reach - holding[i], max(1, budget * portions[i] // whole), spare)
            holding[i] = holding[i] + extra
            spare = spare - extra
    return np.array(holding)


def bell_draw(rng, shape, width, most, cuts=(), kind=jnp.bfloat16):
    level = levels(rng, shape, cuts, -0.22, 0.18) if cuts else 1.0
    values = jax.random.normal(rng, shape, jnp.float32) * width * level
    return jnp.minimum(jnp.maximum(values, -most), most).astype(kind)


def setup_inputs(seed: int = 0, part: int = 0) -> dict:
    seeds = jax.random.split(jax.random.key(seed), 12)
    own_keys = jax.random.split(jax.random.fold_in(seeds[11], part), 12)
    queries = draw_queries(jax.random.fold_in(jax.random.fold_in(seeds[11], part), 71), part)
    keys = draw_keys(jax.random.fold_in(jax.random.fold_in(seeds[11], part), 71), part)
    values = bell_draw(own_keys[2], (NSEQ, SEQ, KVH * HD), 2.0, 12.0, ((0, 2), (1, 8), (2, 2)))
    segments = jax.vmap(lambda own: jnp.searchsorted(jnp.cumsum(ragged(own, SEQ // 32, SEQ, SEQ // 8, 2)), jnp.arange(SEQ), side="right"))(jax.random.split(own_keys[3], NSEQ)).reshape((NSEQ, SEQ)).astype(jnp.int32)
    resid = bell_draw(own_keys[4], (NSEQ, SEQ, D), 1.0, 6.0, ((0, 2), (1, 8), (2, 2)))
    output_weight = bell_draw(seeds[5], (QH * HD, D), (QH * HD // 8) ** -0.5, 0.375, ((0, 2), (1, 2)))
    norm_gain = jnp.clip(1.0 + 0.1 * jax.random.normal(seeds[6], (D,), jnp.float32), 0.5, 1.5)
    routes_keys = jax.random.split(jax.random.fold_in(own_keys[7], 1), NSEQ * SEQ // TOK_DEV)
    routes_turns = jax.random.permutation(jax.random.fold_in(own_keys[7], 3), NSEQ * SEQ // TOK_DEV)
    routes = jax.vmap(lambda own, number: assign_block(jax.random.fold_in(own_keys[7], 2), own, number, TOK_DEV, EXPERTS, TOP, CAP, 2))(routes_keys, routes_turns).reshape((NSEQ, SEQ, TOP))
    route_weights = jnp.clip(0.05 + 0.25 * jax.random.uniform(own_keys[8], (NSEQ, SEQ, TOP), jnp.float32) ** levels(own_keys[8], (NSEQ, SEQ, TOP), ((0, 2), (1, 8)), -0.2, 0.2), 0.05, 0.3)
    w_gu = bell_draw(seeds[9], (EXPERTS, D, 2 * FF), D ** -0.5, 0.125, ((0, 16), (1, 2)))
    w_down = bell_draw(seeds[10], (EXPERTS, FF, D), FF ** -0.5, 0.3125, ((0, 16), (2, 2)))
    return dict(queries=queries, keys=keys, values=values, segments=segments, resid=resid, output_weight=output_weight, norm_gain=norm_gain, routes=routes, route_weights=route_weights, w_gu=w_gu, w_down=w_down)


masked_score = -1e+30
epsilon = 1e-06

def attend_sequence(packed):
    query_seq, key_seq, value_seq, segment_row = packed
    grouped = query_seq.astype(jnp.float32).reshape(SEQ, KVH, QH // KVH, HD)
    key_heads = key_seq.astype(jnp.float32).reshape(SEQ, KVH, HD)
    value_heads = value_seq.astype(jnp.float32).reshape(SEQ, KVH, HD)
    scores = jnp.einsum('tkgd,nkd->kgtn', grouped, key_heads) * (1.0 / math.sqrt(HD))
    allowed = segment_row[None, :] <= segment_row[:, None]
    scores = jnp.where(allowed, scores, masked_score)
    top_score = lax.optimization_barrier(jnp.max(scores, axis=-1, keepdims=True))
    exp_scores = jnp.where(allowed, jnp.exp(scores - top_score), 0.0)
    denominator = lax.optimization_barrier(jnp.sum(exp_scores, axis=-1))
    rounded = lax.optimization_barrier(exp_scores.astype(jnp.bfloat16))
    summed = jnp.einsum('kgtn,nkd->kgtd', rounded.astype(jnp.float32), value_heads)
    attended = (summed / denominator[..., None]).transpose(2, 0, 1, 3).reshape(SEQ, QH * HD)
    return attended.astype(jnp.bfloat16)

def reference(queries, keys, values, segments, resid, output_weight, norm_gain, routes, route_weights, w_gu, w_down):
    attended = lax.map(attend_sequence, (queries, keys, values, segments))
    row_count = NSEQ * SEQ
    projected = jnp.dot(attended.reshape(row_count, QH * HD), output_weight, preferred_element_type=jnp.float32)
    hidden_in = resid.reshape(row_count, D).astype(jnp.float32) + projected
    inv_rms = lax.rsqrt(lax.optimization_barrier(jnp.mean(hidden_in * hidden_in, axis=-1)) + epsilon)
    normed = (hidden_in * inv_rms[:, None] * norm_gain).astype(jnp.bfloat16)
    halves = D // N_HEAD
    normed_blocks = normed.reshape(row_count, N_HEAD, halves)
    flat_routes = routes.reshape(-1)
    flat_weights = route_weights.reshape(-1).astype(jnp.float32)
    most = N_TM * N_EXPERT * CAP

    def single_expert(mixed, expert):
        hits = flat_routes == expert
        picks = jnp.nonzero(hits, size=most, fill_value=0)[0].astype(jnp.int32)
        live = jnp.arange(most, dtype=jnp.int32) < jnp.sum(hits.astype(jnp.int32))
        token_rows = picks // TOP
        input_values = normed_blocks[token_rows].astype(jnp.float32)
        weight_tiles = w_gu[expert].astype(jnp.float32).reshape(N_HEAD, halves, 2 * FF)
        fragments = jnp.einsum('jyl,ylz->jyz', input_values, weight_tiles).astype(jnp.bfloat16)
        fragments = lax.optimization_barrier(fragments)
        gate_up = lax.optimization_barrier(jnp.sum(fragments.astype(jnp.float32), axis=1))
        activated = (jax.nn.silu(gate_up[:, :FF]) * gate_up[:, FF:]).astype(jnp.bfloat16)
        expert_out = jnp.dot(activated, w_down[expert], preferred_element_type=jnp.float32).astype(jnp.bfloat16)
        scaled = jnp.where(live[:, None], expert_out.astype(jnp.float32) * flat_weights[picks][:, None], 0.0)
        return (mixed.at[token_rows].add(scaled), None)
    mixed, unused = lax.scan(single_expert, jnp.zeros((row_count, D), jnp.float32), jnp.arange(EXPERTS, dtype=jnp.int32))
    layer_out = (hidden_in + mixed).astype(jnp.bfloat16)
    return layer_out.reshape(NSEQ, SEQ, D)
```

```python
import math

import jax
import jax.numpy as jnp
from jax import lax
from jax.experimental import pallas as pl
from jax.experimental.pallas import tpu as pltpu
from jax.sharding import PartitionSpec as P

masked_score = -1e30
epsilon = 1e-06
MESH = pl.DeviceIdType.MESH


def deliver(buffer):
    return lax.all_to_all(buffer, ("tm", "expert"), split_axis=0, concat_axis=0, tiled=True)


def local(
    queries,
    keys,
    values,
    segments,
    resid,
    output_weight,
    norm_gain,
    routes,
    route_weights,
    w_gu,
    w_down,
):
    head_size = keys.shape[2]
    tokens = queries.shape[1]
    groups = queries.shape[2] // head_size
    query_blk = queries[0].reshape(tokens, groups, head_size)
    seq_ids = segments[0]
    query_ids = lax.dynamic_slice_in_dim(seq_ids, lax.axis_index("tm") * tokens, tokens)
    score_scale = 1.0 / math.sqrt(head_size)
    running = jnp.full((groups, tokens), masked_score, jnp.float32)
    key_blk = lax.all_gather(keys, "tm", axis=1, tiled=True)[0]
    value_blk = lax.all_gather(values, "tm", axis=1, tiled=True)[0]
    scores = (
        jnp.einsum("tgd,nd->gtn", query_blk, key_blk, preferred_element_type=jnp.float32)
        * score_scale
    )
    allowed = seq_ids[None, None, :] <= query_ids[None, :, None]
    scores = jnp.where(allowed, scores, masked_score)
    newmax = jnp.maximum(running, jnp.max(scores, axis=-1))
    exp_scores = jnp.where(allowed, jnp.exp(scores - newmax[..., None]), 0.0)
    total = jnp.sum(exp_scores, axis=-1)
    weighted = jnp.einsum(
        "gtn,nd->gtd",
        exp_scores.astype(jnp.bfloat16),
        value_blk,
        preferred_element_type=jnp.float32,
    )
    running, total, weighted = (newmax, total, weighted)
    attended = (
        (weighted / total[..., None])
        .transpose(1, 0, 2)
        .reshape(tokens, groups * head_size)
        .astype(jnp.bfloat16)
    )
    partial_value = jnp.dot(
        attended,
        lax.all_gather(output_weight, "expert", axis=1, tiled=True),
        preferred_element_type=jnp.float32,
    )
    width = resid.shape[2]
    full_width = partial_value.shape[1]
    offset = lax.axis_index("head") * width
    placed = lax.dynamic_update_slice_in_dim(
        jnp.zeros((tokens, full_width), jnp.float32), resid[0].astype(jnp.float32), offset, 1
    )
    hidden_in = lax.psum((partial_value + placed).astype(jnp.bfloat16), "head").astype(jnp.float32)
    inv_rms = lax.rsqrt(jnp.mean(hidden_in * hidden_in, axis=-1) + epsilon)
    hidden_half = lax.dynamic_slice_in_dim(hidden_in, offset, width, 1)
    normed_half = (hidden_half * inv_rms[:, None] * norm_gain).astype(jnp.bfloat16)
    expert_total = lax.axis_size("tm") * lax.axis_size("expert")
    top_count = routes.shape[2]
    capacity = min(tokens, 3 * tokens * top_count // (2 * expert_total))
    flat_routes = routes[0].reshape(-1)
    flat_weights = route_weights[0].reshape(-1)
    onehot = (flat_routes[:, None] == jnp.arange(expert_total, dtype=jnp.int32)[None, :]).astype(
        jnp.int32
    )
    earlier = jnp.cumsum(onehot, axis=0) - onehot
    rank = jnp.sum(earlier * onehot, axis=1)
    slot_ids = flat_routes * capacity + rank
    slot_range = jnp.arange(expert_total * capacity, dtype=jnp.int32)
    pair_match = slot_range[:, None] == slot_ids[None, :]
    dispatch = jnp.sum(
        pair_match.reshape(expert_total * capacity, tokens, top_count).astype(jnp.float32), axis=2
    )
    send_rows = jnp.dot(
        dispatch.astype(jnp.bfloat16), normed_half, preferred_element_type=jnp.float32
    ).astype(jnp.bfloat16)
    arrived = deliver(send_rows.reshape(expert_total, capacity, width))
    arrived_rows = arrived.reshape(expert_total * capacity, width)
    block_gate = jnp.dot(arrived_rows, w_gu[0], preferred_element_type=jnp.float32).astype(
        jnp.bfloat16
    )
    gate_up = lax.psum(block_gate, "head").astype(jnp.float32)
    feedforward_count = w_down.shape[1]
    activated = (
        jax.nn.silu(gate_up[:, :feedforward_count]) * gate_up[:, feedforward_count:]
    ).astype(jnp.bfloat16)
    expert_out = jnp.dot(activated, w_down[0], preferred_element_type=jnp.float32).astype(
        jnp.bfloat16
    )
    returned = deliver(expert_out.reshape(expert_total, capacity, width))
    returned_rows = returned.reshape(expert_total * capacity, width).astype(jnp.float32)
    combine = jnp.sum(
        (pair_match.astype(jnp.float32) * flat_weights[None, :]).reshape(
            expert_total * capacity, tokens, top_count
        ),
        axis=2,
    )
    mixed = jnp.dot(combine.T, returned_rows, precision=lax.Precision.HIGHEST)
    layer_out = (hidden_half + mixed).astype(jnp.bfloat16)
    return layer_out[None]


def fused_kernel(
    q_ref,
    k_ref,
    v_ref,
    seg_ref,
    resid_ref,
    ow_ref,
    gain_ref,
    routes_ref,
    rw_ref,
    wgu_ref,
    wdn_ref,
    out_ref,
    kv,
    coef,
    attended,
    core_send,
    core_recv,
    diag_send,
    diag_recv,
    projected,
    squares,
    hidden,
    rows,
    gu_other,
    dn_other,
    part_send,
    part_recv,
    y_send,
    y_recv,
    z_send,
    z_recv,
    kept,
    kv_ss,
    kv_rs,
    coef_ss,
    coef_rs,
    row_ss,
    row_rs,
    w_ss,
    w_rs,
    att_ss,
    att_rs,
    mid_ss,
    mid_rs,
    part_ss,
    part_rs,
    y_ss,
    y_rs,
    z_ss,
    z_rs,
):
    f32, bf16 = jnp.float32, jnp.bfloat16
    tm = lax.axis_index("tm")
    x = lax.axis_index("expert")
    h = lax.axis_index("head")
    z, y = tm // 2, tm % 2
    far = [z, z + 1 - 2 * (z % 2), (z + 2) % 4, 3 - z]
    to_y = {"tm": z * 2 + 1 - y}
    to_z = [None] + [{"tm": far[d] * 2 + y} for d in (1, 2, 3)]
    to_x = {"expert": 1 - x}
    to_core = {"head": 1 - h}
    to_diag = {"expert": 1 - x, "head": 1 - h}
    tokens = q_ref.shape[0]
    hd = k_ref.shape[1]
    heads = q_ref.shape[1] // hd
    width = resid_ref.shape[1]
    ff = wdn_ref.shape[0]
    experts = coef.shape[0] // 8

    def remote(src, dst, ss, rs, dev):
        return pltpu.make_async_remote_copy(
            src_ref=src, dst_ref=dst, send_sem=ss, recv_sem=rs, device_id=dev, device_id_type=MESH
        )

    def spread(at, ss, rs):
        copies = {1: remote(at(0), at(1), ss.at[1], rs.at[1], to_y)}
        for d in (1, 2, 3):
            copies[2 * d] = remote(at(0), at(2 * d), ss.at[2 * d], rs.at[2 * d], to_z[d])
            copies[2 * d + 1] = remote(
                at(2 * d), at(2 * d + 1), ss.at[2 * d + 1], rs.at[2 * d + 1], to_y
            )
        return copies

    barrier = pltpu.get_barrier_semaphore()
    peers = [to_y, to_z[1], to_z[2], to_z[3], to_x, to_core, to_diag]
    for dev in peers:
        pl.semaphore_signal(barrier, inc=1, device_id=dev, device_id_type=MESH)

    kv[0, 0] = k_ref[...]
    kv[0, 1] = v_ref[...]
    lanes = lax.broadcasted_iota(jnp.int32, (tokens, 128), 1)
    dense = jnp.zeros((tokens, 128), f32)
    for k in range(routes_ref.shape[1]):
        dense += jnp.where(lanes == routes_ref[:, k : k + 1], rw_ref[:, k : k + 1], 0.0)
    coef[0:experts, :] = dense.T[0:experts, :]

    pl.semaphore_wait(barrier, len(peers))

    kv_at = lambda s: kv.at[s]
    kv_copies = spread(kv_at, kv_ss, kv_rs)
    coef_copies = spread(lambda s: coef.at[pl.ds(s * experts, experts)], coef_ss, coef_rs)
    row_copies = spread(lambda s: rows.at[s], row_ss, row_rs)
    for s in (1, 2, 4, 6):
        kv_copies[s].start()
    half = wgu_ref.shape[0] // 2
    w_copies = [
        remote(wgu_ref.at[pl.ds(0, half)], gu_other.at[pl.ds(0, half)], w_ss.at[0], w_rs.at[0], to_x),
        remote(
            wgu_ref.at[pl.ds(half, half)], gu_other.at[pl.ds(half, half)], w_ss.at[1], w_rs.at[1], to_x
        ),
        remote(wdn_ref, dn_other, w_ss.at[2], w_rs.at[2], to_x),
    ]
    w_copies[0].start()
    for s in (1, 2, 4, 6):
        coef_copies[s].start()
    for d in (1, 2, 3):
        kv_copies[2 * d].wait_recv()
        kv_copies[2 * d + 1].start()
    for d in (1, 2, 3):
        coef_copies[2 * d].wait_recv()
        coef_copies[2 * d + 1].start()
    for s in (1, 3, 5, 7):
        kv_copies[s].wait_recv()

    own_ids = seg_ref[:, pl.ds(pl.multiple_of(tm * tokens, tokens), tokens)].astype(f32)
    own_column = jnp.broadcast_to(own_ids, (tokens, tokens)).T
    allowed = []
    for s in range(8):
        place = far[s // 2] * 2 + (y if s % 2 == 0 else 1 - y)
        ids = seg_ref[:, pl.ds(pl.multiple_of(place * tokens, tokens), tokens)].astype(f32)
        allowed.append(jnp.broadcast_to(ids, (tokens, tokens)) <= own_column)
    allowed = jnp.concatenate(
        [jnp.where(a, 0.0, masked_score) for a in allowed], axis=1
    )
    key_all = kv[:, 0].reshape(8 * tokens, hd)
    value_all = kv[:, 1].reshape(8 * tokens, hd)
    scale = 1.0 / math.sqrt(hd)
    att_copies = []
    for g in range(heads):
        cols = pl.ds(g * hd, hd)
        scores = lax.dot_general(
            q_ref[:, cols], key_all, (((1,), (1,)), ((), ())), preferred_element_type=f32
        )
        scores = jnp.where(allowed < 0.0, masked_score, scores * scale)
        top = jnp.max(scores, axis=1, keepdims=True)
        probs = jnp.exp(scores - top)
        total = jnp.sum(probs, axis=1, keepdims=True)
        summed = jnp.dot(probs.astype(bf16), value_all, preferred_element_type=f32)
        attended[x, :, cols] = (summed / total).astype(bf16)
        if g % 2 == 1:
            pair = pl.ds((g - 1) * hd, 2 * hd)
            here = attended.at[x, :, pair]
            copy = remote(here, here, att_ss.at[g // 2], att_rs.at[g // 2], to_x)
            copy.start()
            att_copies.append(copy)
    for copy in att_copies:
        copy.wait()

    core_send[...] = jnp.dot(
        attended[1 - h], ow_ref[...], preferred_element_type=f32
    ).astype(bf16)
    core_copy = remote(core_send, core_recv, mid_ss.at[0], mid_rs.at[0], to_core)
    core_copy.start()
    projected[...] = jnp.dot(attended[h], ow_ref[...], preferred_element_type=f32)
    core_copy.wait()
    projected[...] += core_recv[...].astype(f32)

    @pl.when(x != h)
    def _():
        diag_send[...] = projected[...].astype(bf16)
        diag_copy = remote(diag_send, diag_recv, mid_ss.at[1], mid_rs.at[1], to_diag)
        diag_copy.start()
        diag_copy.wait()
        projected[...] = diag_recv[...].astype(f32)

    w_copies[1].start()
    w_copies[2].start()

    hidden[...] = projected[...] + resid_ref[...].astype(f32)
    own_sum = jnp.sum(hidden[...] * hidden[...], axis=1, keepdims=True)
    squares[0] = jnp.broadcast_to(own_sum, (tokens, 128))
    sq_copy = remote(squares.at[0], squares.at[1], mid_ss.at[2], mid_rs.at[2], to_core)
    sq_copy.start()
    sq_copy.wait()
    mean = (squares[0][:, 0:1] + squares[1][:, 0:1]) * (1.0 / (2 * width))
    rows[0] = (hidden[...] * lax.rsqrt(mean + epsilon) * gain_ref[...]).astype(bf16)
    for s in (1, 2, 4, 6):
        row_copies[s].start()
    for s in (1, 3, 5, 7):
        coef_copies[s].wait_recv()
    by_token = coef[...].T

    part_copies = [[None] * 8, [None] * 8]

    def gate_up(s, which, weights):
        part_send[which, s] = jnp.dot(
            rows[s], weights[...], preferred_element_type=f32
        ).astype(bf16)
        copy = remote(
            part_send.at[which, s],
            part_recv.at[which, s],
            part_ss.at[which, s],
            part_rs.at[which, s],
            to_core,
        )
        copy.start()
        part_copies[which][s] = copy

    gate_up(0, 0, wgu_ref)
    for s in (1, 2, 3, 4, 5, 6, 7):
        row_copies[s].wait_recv()
        if s % 2 == 0:
            row_copies[s + 1].start()
        gate_up(s, 0, wgu_ref)

    w_copies[0].wait_recv()
    w_copies[1].wait_recv()
    w_copies[2].wait_recv()
    mine = tm * 2 + x
    theirs = tm * 2 + 1 - x

    def expert(s, which, weights, index):
        part_copies[which][s].wait_recv()
        both = part_send[which, s].astype(f32) + part_recv[which, s].astype(f32)
        gate, up = both[:, :ff], both[:, ff:]
        act = (gate / (1.0 + jnp.exp(-gate)) * up).astype(bf16)
        down = jnp.dot(act, weights[...], preferred_element_type=f32).astype(bf16).astype(f32)
        wanted = jnp.where(lanes == s * experts + index, by_token, 0.0)
        return down * jnp.sum(wanted, axis=1, keepdims=True)

    y_copies, z_copies = {}, {}

    def finish(s):
        mixed = expert(s, 0, wdn_ref, mine) + expert(s, 1, dn_other, theirs)
        d = s // 2
        if s % 2 == 1:
            y_send[d] = mixed.astype(bf16)
            copy = remote(y_send.at[d], y_recv.at[d], y_ss.at[d], y_rs.at[d], to_y)
            copy.start()
            y_copies[d] = copy
        else:
            kept[d] = mixed

    def pass_on(d):
        y_copies[d].wait_recv()
        if d == 0:
            kept[0] = kept[0] + y_recv[0].astype(f32)
            return
        z_send[d - 1] = (kept[d] + y_recv[d].astype(f32)).astype(bf16)
        copy = remote(
            z_send.at[d - 1], z_recv.at[d - 1], z_ss.at[d - 1], z_rs.at[d - 1], to_z[d]
        )
        copy.start()
        z_copies[d] = copy

    order = [7, 6, 5, 4, 3, 2, 1, 0]
    gate_up(order[0], 1, gu_other)
    for i, s in enumerate(order):
        if i + 1 < 8:
            gate_up(order[i + 1], 1, gu_other)
        finish(s)
        if s % 2 == 1 and s < 7:
            pass_on(s // 2 + 1)
    pass_on(0)
    total = hidden[...] + kept[0]
    for d in (3, 2, 1):
        z_copies[d].wait_recv()
        total += z_recv[d - 1].astype(f32)
    out_ref[...] = total.astype(bf16)

    for s in range(1, 8):
        kv_copies[s].wait_send()
        coef_copies[s].wait_send()
        row_copies[s].wait_send()
    for copy in w_copies:
        copy.wait_send()
    for which in range(2):
        for s in range(8):
            part_copies[which][s].wait_send()
    for d in range(4):
        y_copies[d].wait_send()
    for d in (1, 2, 3):
        z_copies[d].wait_send()


def fused(
    queries,
    keys,
    values,
    segments,
    resid,
    output_weight,
    norm_gain,
    routes,
    route_weights,
    w_gu,
    w_down,
):
    bf16, f32 = jnp.bfloat16, jnp.float32
    tokens, width = resid.shape[1:]
    hd = keys.shape[2]
    ff = w_down.shape[1]
    experts = lax.axis_size("tm") * lax.axis_size("expert")
    block = (tokens, width)
    dma = pltpu.SemaphoreType.DMA
    out = pl.pallas_call(
        fused_kernel,
        out_shape=jax.ShapeDtypeStruct(block, bf16),
        in_specs=[pl.BlockSpec(memory_space=pltpu.VMEM)] * 11,
        out_specs=pl.BlockSpec(memory_space=pltpu.VMEM),
        scratch_shapes=[
            pltpu.VMEM((8, 2, tokens, hd), bf16),
            pltpu.VMEM((8 * experts, tokens), f32),
            pltpu.VMEM((2, tokens, queries.shape[2]), bf16),
            pltpu.VMEM((tokens, output_weight.shape[1]), bf16),
            pltpu.VMEM((tokens, output_weight.shape[1]), bf16),
            pltpu.VMEM(block, bf16),
            pltpu.VMEM(block, bf16),
            pltpu.VMEM(block, f32),
            pltpu.VMEM((2, tokens, 128), f32),
            pltpu.VMEM(block, f32),
            pltpu.VMEM((8,) + block, bf16),
            pltpu.VMEM(w_gu.shape[1:], bf16),
            pltpu.VMEM(w_down.shape[1:], bf16),
            pltpu.VMEM((2, 8, tokens, 2 * ff), bf16),
            pltpu.VMEM((2, 8, tokens, 2 * ff), bf16),
            pltpu.VMEM((4,) + block, bf16),
            pltpu.VMEM((4,) + block, bf16),
            pltpu.VMEM((3,) + block, bf16),
            pltpu.VMEM((3,) + block, bf16),
            pltpu.VMEM((4,) + block, f32),
            dma((8,)),
            dma((8,)),
            dma((8,)),
            dma((8,)),
            dma((8,)),
            dma((8,)),
            dma((3,)),
            dma((3,)),
            dma((4,)),
            dma((4,)),
            dma((3,)),
            dma((3,)),
            dma((2, 8)),
            dma((2, 8)),
            dma((4,)),
            dma((4,)),
            dma((3,)),
            dma((3,)),
        ],
        compiler_params=pltpu.CompilerParams(
            collective_id=0, has_side_effects=True, vmem_limit_bytes=56 * 2**20
        ),
    )(
        queries[0],
        keys[0],
        values[0],
        segments,
        resid[0],
        output_weight,
        norm_gain[None],
        routes[0],
        route_weights[0],
        w_gu[0],
        w_down[0],
    )
    return out[None]


def solution(mesh):
    placed = (
        P(("groups", "expert"), "tm", "head"),
        P(("groups", "expert"), "tm", "head"),
        P(("groups", "expert"), "tm", "head"),
        P(("groups", "expert"), None),
        P(("groups", "expert"), "tm", "head"),
        P("head", "expert"),
        P("head"),
        P(("groups", "expert"), "tm", None),
        P(("groups", "expert"), "tm", None),
        P(("tm", "expert"), "head", None),
        P(("tm", "expert"), None, "head"),
    )
    sizes = mesh.shape
    few = (sizes["tm"], sizes["expert"], sizes["head"]) == (8, 2, 2)
    return jax.shard_map(
        fused if few else local,
        mesh=mesh,
        in_specs=placed,
        out_specs=P(("groups", "expert"), "tm", "head"),
        check_vma=False,
    )
```

```python
import math

import jax
import jax.numpy as jnp
from jax import lax
from jax.experimental import pallas as pl
from jax.experimental.pallas import tpu as pltpu
from jax.sharding import PartitionSpec as P

masked_score = -1e30
epsilon = 1e-06
MESH = pl.DeviceIdType.MESH


def deliver(buffer):
    return lax.all_to_all(buffer, ("tm", "expert"), split_axis=0, concat_axis=0, tiled=True)


def local(
    queries,
    keys,
    values,
    segments,
    resid,
    output_weight,
    norm_gain,
    routes,
    route_weights,
    w_gu,
    w_down,
):
    head_size = keys.shape[2]
    tokens = queries.shape[1]
    groups = queries.shape[2] // head_size
    query_blk = queries[0].reshape(tokens, groups, head_size)
    seq_ids = segments[0]
    query_ids = lax.dynamic_slice_in_dim(seq_ids, lax.axis_index("tm") * tokens, tokens)
    score_scale = 1.0 / math.sqrt(head_size)
    running = jnp.full((groups, tokens), masked_score, jnp.float32)
    key_blk = lax.all_gather(keys, "tm", axis=1, tiled=True)[0]
    value_blk = lax.all_gather(values, "tm", axis=1, tiled=True)[0]
    scores = (
        jnp.einsum("tgd,nd->gtn", query_blk, key_blk, preferred_element_type=jnp.float32)
        * score_scale
    )
    allowed = seq_ids[None, None, :] <= query_ids[None, :, None]
    scores = jnp.where(allowed, scores, masked_score)
    newmax = jnp.maximum(running, jnp.max(scores, axis=-1))
    exp_scores = jnp.where(allowed, jnp.exp(scores - newmax[..., None]), 0.0)
    total = jnp.sum(exp_scores, axis=-1)
    weighted = jnp.einsum(
        "gtn,nd->gtd",
        exp_scores.astype(jnp.bfloat16),
        value_blk,
        preferred_element_type=jnp.float32,
    )
    running, total, weighted = (newmax, total, weighted)
    attended = (
        (weighted / total[..., None])
        .transpose(1, 0, 2)
        .reshape(tokens, groups * head_size)
        .astype(jnp.bfloat16)
    )
    partial_value = jnp.dot(
        attended,
        lax.all_gather(output_weight, "expert", axis=1, tiled=True),
        preferred_element_type=jnp.float32,
    )
    width = resid.shape[2]
    full_width = partial_value.shape[1]
    offset = lax.axis_index("head") * width
    placed = lax.dynamic_update_slice_in_dim(
        jnp.zeros((tokens, full_width), jnp.float32), resid[0].astype(jnp.float32), offset, 1
    )
    hidden_in = lax.psum((partial_value + placed).astype(jnp.bfloat16), "head").astype(jnp.float32)
    inv_rms = lax.rsqrt(jnp.mean(hidden_in * hidden_in, axis=-1) + epsilon)
    hidden_half = lax.dynamic_slice_in_dim(hidden_in, offset, width, 1)
    normed_half = (hidden_half * inv_rms[:, None] * norm_gain).astype(jnp.bfloat16)
    expert_total = lax.axis_size("tm") * lax.axis_size("expert")
    top_count = routes.shape[2]
    capacity = min(tokens, 3 * tokens * top_count // (2 * expert_total))
    flat_routes = routes[0].reshape(-1)
    flat_weights = route_weights[0].reshape(-1)
    onehot = (flat_routes[:, None] == jnp.arange(expert_total, dtype=jnp.int32)[None, :]).astype(
        jnp.int32
    )
    earlier = jnp.cumsum(onehot, axis=0) - onehot
    rank = jnp.sum(earlier * onehot, axis=1)
    slot_ids = flat_routes * capacity + rank
    slot_range = jnp.arange(expert_total * capacity, dtype=jnp.int32)
    pair_match = slot_range[:, None] == slot_ids[None, :]
    dispatch = jnp.sum(
        pair_match.reshape(expert_total * capacity, tokens, top_count).astype(jnp.float32), axis=2
    )
    send_rows = jnp.dot(
        dispatch.astype(jnp.bfloat16), normed_half, preferred_element_type=jnp.float32
    ).astype(jnp.bfloat16)
    arrived = deliver(send_rows.reshape(expert_total, capacity, width))
    arrived_rows = arrived.reshape(expert_total * capacity, width)
    block_gate = jnp.dot(arrived_rows, w_gu[0], preferred_element_type=jnp.float32).astype(
        jnp.bfloat16
    )
    gate_up = lax.psum(block_gate, "head").astype(jnp.float32)
    feedforward_count = w_down.shape[1]
    activated = (
        jax.nn.silu(gate_up[:, :feedforward_count]) * gate_up[:, feedforward_count:]
    ).astype(jnp.bfloat16)
    expert_out = jnp.dot(activated, w_down[0], preferred_element_type=jnp.float32).astype(
        jnp.bfloat16
    )
    returned = deliver(expert_out.reshape(expert_total, capacity, width))
    returned_rows = returned.reshape(expert_total * capacity, width).astype(jnp.float32)
    combine = jnp.sum(
        (pair_match.astype(jnp.float32) * flat_weights[None, :]).reshape(
            expert_total * capacity, tokens, top_count
        ),
        axis=2,
    )
    mixed = jnp.dot(combine.T, returned_rows, precision=lax.Precision.HIGHEST)
    layer_out = (hidden_half + mixed).astype(jnp.bfloat16)
    return layer_out[None]


def fused_kernel(
    q_ref,
    k_ref,
    v_ref,
    seg_ref,
    resid_hbm,
    ow_hbm,
    gain_ref,
    routes_ref,
    rw_ref,
    wgu_hbm,
    wdn_hbm,
    out_ref,
    kv,
    coef,
    attended,
    core_send,
    core_recv,
    diag_send,
    diag_recv,
    projected,
    squares,
    hidden,
    rows,
    resid_ref,
    ow_ref,
    gu_own,
    gu_other,
    down,
    acts,
    part_send,
    part_recv,
    y_send,
    y_recv,
    z_send,
    z_recv,
    kept,
    kv_ss,
    kv_rs,
    coef_ss,
    coef_rs,
    row_ss,
    row_rs,
    w_ss,
    w_rs,
    att_ss,
    att_rs,
    mid_ss,
    mid_rs,
    part_ss,
    part_rs,
    y_ss,
    y_rs,
    z_ss,
    z_rs,
    load_sems,
):
    f32, bf16 = jnp.float32, jnp.bfloat16
    tm = lax.axis_index("tm")
    x = lax.axis_index("expert")
    h = lax.axis_index("head")
    z, y = tm // 2, tm % 2
    near = z - 1 + 2 * ((3 - z) // 3)
    last = 3 * (1 - z // 2)
    line = [near, 6 - z - near - last, last]
    to_y = {"tm": z * 2 + 1 - y}
    to_z = [{"tm": u * 2 + y} for u in line]
    to_up, to_down = {"tm": tm + 2}, {"tm": tm - 2}
    to_x = {"expert": 1 - x}
    to_core = {"head": 1 - h}
    to_diag = {"expert": 1 - x, "head": 1 - h}
    tokens = q_ref.shape[0]
    hd = k_ref.shape[1]
    heads = q_ref.shape[1] // hd
    width = resid_ref.shape[1]
    ff = wdn_hbm.shape[0]
    loads = [
        pltpu.make_async_copy(src, dst, load_sems.at[i])
        for i, (src, dst) in enumerate(
            [
                (ow_hbm, ow_ref),
                (resid_hbm, resid_ref),
                (wgu_hbm, gu_own),
                (wdn_hbm, down.at[pl.ds(0, ff)]),
            ]
        )
    ]
    for load in loads:
        load.start()
    experts = coef.shape[0] // 8

    def remote(src, dst, ss, rs, dev):
        return pltpu.make_async_remote_copy(
            src_ref=src, dst_ref=dst, send_sem=ss, recv_sem=rs, device_id=dev, device_id_type=MESH
        )

    class Spread:
        def __init__(self, at, chunks, ss, rs):
            self.at, self.chunks, self.ss, self.rs = at, chunks, ss, rs

        def copies(self, u, c):
            slot = 2 * u + y
            here = self.at(slot, c)
            rs = self.rs.at[slot, c]
            return [
                remote(here, here, self.ss.at[way, u, c], rs, dev)
                for way, dev in enumerate((to_up, to_down, to_y))
            ]

        def send(self, u, c):
            up, down, across = self.copies(u, c)
            pl.when((z < 3) & (u <= z))(up.start)
            pl.when((z > 0) & (u >= z))(down.start)
            across.start()

        def arrive(self, slot, c):
            here = self.at(slot, c)
            remote(here, here, self.ss.at[2, 0, c], self.rs.at[slot, c], to_y).wait_recv()

        def begin(self):
            for c in range(self.chunks):
                self.send(z, c)

        def relay(self, u, c):
            self.arrive(2 * u + y, c)
            self.send(u, c)

        def finish(self):
            for u in range(4):
                for c in range(self.chunks):
                    up, down, across = self.copies(u, c)
                    pl.when((z < 3) & (u <= z))(up.wait_send)
                    pl.when((z > 0) & (u >= z))(down.wait_send)
                    across.wait_send()

    class Direct(Spread):
        def copies(self, u, c):
            here = self.at(2 * u + y, c)
            return remote(here, here, self.ss.at[2, u, c], self.rs.at[2 * u + y, c], to_y)

        def sends(self):
            here, rs = self.at(tm, 0), self.rs.at[tm, 0]
            return [remote(here, here, self.ss.at[0, i, 0], rs, to_z[i]) for i in range(3)]

        def begin(self):
            self.copies(z, 0).start()
            for copy in self.sends():
                copy.start()

        def send(self, u, c):
            self.copies(u, c).start()

        def finish(self):
            for u in range(4):
                self.copies(u, 0).wait_send()
            for copy in self.sends():
                copy.wait_send()

    barrier = pltpu.get_barrier_semaphore()
    peers = [to_y, to_x, to_core, to_diag] + to_z
    for dev in peers:
        pl.semaphore_signal(barrier, inc=1, device_id=dev, device_id_type=MESH)

    kv[tm, 0] = k_ref[...]
    kv[tm, 1] = v_ref[...]
    lanes = lax.broadcasted_iota(jnp.int32, (tokens, 128), 1)
    numbers = lax.broadcasted_iota(jnp.int32, (experts, tokens), 0)
    dense = jnp.zeros((experts, tokens), f32)
    for k in range(routes_ref.shape[0]):
        dense += jnp.where(numbers == routes_ref[k : k + 1, :], rw_ref[k : k + 1, :], 0.0)
    coef[pl.ds(tm * experts, experts), :] = dense

    pl.semaphore_wait(barrier, len(peers))

    kv_spread = Direct(lambda s, c: kv.at[s], 1, kv_ss, kv_rs)
    coef_spread = Direct(lambda s, c: coef.at[pl.ds(s * experts, experts)], 1, coef_ss, coef_rs)
    piece = tokens // row_rs.shape[1]
    row_spread = Spread(
        lambda s, c: rows.at[s, pl.ds(c * piece, piece)], row_rs.shape[1], row_ss, row_rs
    )
    kv_spread.begin()
    gu_rows = wgu_hbm.shape[0] // 8
    parts = 2
    part = width // parts
    dn_rows = ff // 2
    w_parts = [
        (wgu_hbm.at[pl.ds(i * gu_rows, gu_rows)], gu_other.at[pl.ds(i * gu_rows, gu_rows)])
        for i in range(8)
    ] + [
        (
            wdn_hbm.at[pl.ds(r * dn_rows, dn_rows), pl.ds(c * part, part)],
            down.at[pl.ds(ff + r * dn_rows, dn_rows), pl.ds(c * part, part)],
        )
        for c in range(parts)
        for r in range(2)
    ]
    w_copies = [
        remote(src, dst, w_ss.at[i], w_rs.at[i], to_x) for i, (src, dst) in enumerate(w_parts)
    ]
    waiting = list(w_copies)

    def some_weights(count):
        for copy in waiting[:count]:
            copy.start()
        del waiting[:count]

    some_weights(3)
    coef_spread.begin()
    for u in line:
        kv_spread.relay(u, 0)
    for u in line:
        coef_spread.relay(u, 0)
    kv_spread.arrive(tm + 1 - 2 * y, 0)
    for u in line:
        kv_spread.arrive(2 * u + 1 - y, 0)

    own_ids = seg_ref[:, pl.ds(pl.multiple_of(tm * tokens, tokens), tokens)].astype(f32)
    own_column = jnp.broadcast_to(own_ids, (tokens, tokens)).T
    all_ids = jnp.broadcast_to(seg_ref[...].astype(f32), (tokens, 8 * tokens))
    allowed = all_ids <= jnp.concatenate([own_column] * 8, axis=1)
    key_all = kv[:, 0].reshape(8 * tokens, hd)
    value_all = kv[:, 1].reshape(8 * tokens, hd)
    scale = 1.0 / math.sqrt(hd)
    pieces = row_spread.chunks
    att_copies = {}
    for c in range(pieces):
        some = pl.ds(c * piece, piece)
        allowed_here = allowed[c * piece : (c + 1) * piece]
        for g in range(heads):
            cols = pl.ds(g * hd, hd)
            scores = lax.dot_general(
                q_ref[some, cols], key_all, (((1,), (1,)), ((), ())), preferred_element_type=f32
            )
            scores = jnp.where(allowed_here, scores * scale, masked_score)
            top = jnp.max(scores, axis=1, keepdims=True)
            probs = jnp.exp(scores - top)
            total = jnp.sum(probs, axis=1, keepdims=True)
            summed = jnp.dot(probs.astype(bf16), value_all, preferred_element_type=f32)
            attended[x, some, cols] = (summed / total).astype(bf16)
            if g % 4 == 3:
                here = attended.at[x, some, pl.ds((g - 3) * hd, 4 * hd)]
                i = c, g // 4
                att_copies[i] = remote(here, here, att_ss.at[i], att_rs.at[i], to_x)
                att_copies[i].start()

    def mid(c, i, src, dst, dev):
        some = pl.ds(c * piece, piece)
        return remote(src.at[some], dst.at[some], mid_ss.at[i, c], mid_rs.at[i, c], dev)

    core_copies = [mid(c, 0, core_send, core_recv, to_core) for c in range(pieces)]
    diag_copies = [mid(c, 1, diag_send, diag_recv, to_diag) for c in range(pieces)]
    sq_copies = [mid(c, 2, squares.at[0], squares.at[1], to_core) for c in range(pieces)]
    loads[0].wait()
    for c in range(pieces):
        some = pl.ds(c * piece, piece)
        for i in range(2):
            att_copies[c, i].wait()
        core_send[some] = jnp.dot(
            attended[1 - h, some], ow_ref[...], preferred_element_type=f32
        ).astype(bf16)
        core_copies[c].start()
        projected[some] = jnp.dot(attended[h, some], ow_ref[...], preferred_element_type=f32)
    some_weights(1)
    for c in range(pieces):
        some = pl.ds(c * piece, piece)
        core_copies[c].wait()
        projected[some] += core_recv[some].astype(f32)
        diag_send[some] = projected[some].astype(bf16)
        pl.when(x != h)(diag_copies[c].start)
    some_weights(2)
    loads[1].wait()
    for c in range(pieces):
        some = pl.ds(c * piece, piece)

        @pl.when(x != h)
        def _():
            diag_copies[c].wait()
            projected[some] = diag_recv[some].astype(f32)

        full = projected[some] + resid_ref[some].astype(f32)
        hidden[some] = full
        own_sum = jnp.sum(full * full, axis=1, keepdims=True)
        squares[0, some] = jnp.broadcast_to(own_sum, (piece, 128))
        sq_copies[c].start()
    for c in range(pieces):
        some = pl.ds(c * piece, piece)
        sq_copies[c].wait()
        mean = (squares[0, some][:, 0:1] + squares[1, some][:, 0:1]) * (1.0 / (2 * width))
        rows[tm, some] = (hidden[some] * lax.rsqrt(mean + epsilon) * gain_ref[...]).astype(bf16)
        row_spread.send(z, c)
    coef_spread.arrive(tm + 1 - 2 * y, 0)
    for u in line:
        coef_spread.arrive(2 * u + 1 - y, 0)
    by_token = coef[...].T

    def part_copy(s, which):
        return remote(
            part_send.at[which, s],
            part_recv.at[which, s],
            part_ss.at[which, s],
            part_rs.at[which, s],
            to_core,
        )

    def gate_up(s, which, weights):
        part_send[which, s] = jnp.dot(
            rows[s], weights[...], preferred_element_type=f32
        ).astype(bf16)
        part_copy(s, which).start()

    loads[2].wait()
    gate_up(tm, 0, gu_own)

    def across(u):
        for c in range(row_spread.chunks):
            row_spread.arrive(2 * u + 1 - y, c)
        gate_up(2 * u + 1 - y, 0, gu_own)

    for i, u in enumerate(line):
        for c in range(row_spread.chunks):
            row_spread.relay(u, c)
            some_weights(1)
        gate_up(2 * u + y, 0, gu_own)
        across(z if i == 0 else line[i - 1])
    across(line[2])

    for copy in w_copies[:8]:
        copy.wait_recv()
    inward = [line[2], line[1], line[0], z]
    order = [2 * u + 1 - y for u in inward] + [2 * u + y for u in inward]
    for s in order:
        gate_up(s, 1, gu_other)

    mine = [tm * 2 + x, tm * 2 + 1 - x]
    for s in order:
        for which in range(2):
            part_copy(s, which).wait_recv()
            both = part_send[which, s].astype(f32) + part_recv[which, s].astype(f32)
            gate, up = both[:, :ff], both[:, ff:]
            wanted = jnp.where(lanes == s * experts + mine[which], by_token, 0.0)
            weight = jnp.sum(wanted, axis=1, keepdims=True)
            acts[s, :, which * ff : (which + 1) * ff] = (
                gate / (1.0 + jnp.exp(-gate)) * up * weight
            ).astype(bf16)

    def y_copy(u, c):
        cols = pl.ds(c * part, part)
        return remote(y_send.at[u, :, cols], y_recv.at[u, :, cols], y_ss.at[u, c], y_rs.at[u, c], to_y)

    def z_copy(u, c, mine):
        cols = pl.ds(c * part, part)
        slot = z if mine else u
        return remote(
            z_send.at[u, :, cols],
            z_recv.at[slot, :, cols],
            z_ss.at[u, c],
            z_rs.at[slot, c],
            {"tm": u * 2 + y},
        )

    def pass_on(u, c):
        cols = pl.ds(c * part, part)
        y_copy(u, c).wait_recv()
        z_send[u, :, cols] = (kept[u, :, cols] + y_recv[u, :, cols].astype(f32)).astype(bf16)
        z_copy(u, c, True).start()

    loads[3].wait()
    for c in range(parts):
        cols = pl.ds(c * part, part)
        for copy in w_copies[8 + 2 * c : 10 + 2 * c]:
            copy.wait_recv()
        for i, s in enumerate(order):
            u = inward[i % 4]
            mixed = jnp.dot(acts[s], down[:, cols], preferred_element_type=f32)
            if i >= 4:
                kept[u, :, cols] = mixed
                continue
            y_send[u, :, cols] = mixed.astype(bf16)
            y_copy(u, c).start()
    for c in range(parts):
        for u in inward[:3]:
            pass_on(u, c)
    for c in range(parts):
        cols = pl.ds(c * part, part)
        y_copy(z, c).wait_recv()
        mixed = hidden[:, cols] + kept[z, :, cols] + y_recv[z, :, cols].astype(f32)
        for u in inward[:3]:
            z_copy(u, c, False).wait_recv()
            mixed += z_recv[u, :, cols].astype(f32)
        out_ref[:, cols] = mixed.astype(bf16)

    for spread in (kv_spread, coef_spread, row_spread):
        spread.finish()
    for copy in w_copies:
        copy.wait_send()
    for s in range(8):
        for which in range(2):
            part_copy(s, which).wait_send()
    for u in range(4):
        for c in range(parts):
            y_copy(u, c).wait_send()
    for u in line:
        for c in range(parts):
            z_copy(u, c, True).wait_send()


def fused(
    queries,
    keys,
    values,
    segments,
    resid,
    output_weight,
    norm_gain,
    routes,
    route_weights,
    w_gu,
    w_down,
):
    bf16, f32 = jnp.bfloat16, jnp.float32
    tokens, width = resid.shape[1:]
    hd = keys.shape[2]
    ff = w_down.shape[1]
    experts = lax.axis_size("tm") * lax.axis_size("expert")
    block = (tokens, width)
    dma = pltpu.SemaphoreType.DMA
    out = pl.pallas_call(
        fused_kernel,
        out_shape=jax.ShapeDtypeStruct(block, bf16),
        in_specs=[
            pl.BlockSpec(memory_space=pl.ANY if i in (4, 5, 9, 10) else pltpu.VMEM)
            for i in range(11)
        ],
        out_specs=pl.BlockSpec(memory_space=pltpu.VMEM),
        scratch_shapes=[
            pltpu.VMEM((8, 2, tokens, hd), bf16),
            pltpu.VMEM((8 * experts, tokens), f32),
            pltpu.VMEM((2, tokens, queries.shape[2]), bf16),
            pltpu.VMEM((tokens, output_weight.shape[1]), bf16),
            pltpu.VMEM((tokens, output_weight.shape[1]), bf16),
            pltpu.VMEM(block, bf16),
            pltpu.VMEM(block, bf16),
            pltpu.VMEM(block, f32),
            pltpu.VMEM((2, tokens, 128), f32),
            pltpu.VMEM(block, f32),
            pltpu.VMEM((8,) + block, bf16),
            pltpu.VMEM(block, bf16),
            pltpu.VMEM(output_weight.shape, bf16),
            pltpu.VMEM(w_gu.shape[1:], bf16),
            pltpu.VMEM(w_gu.shape[1:], bf16),
            pltpu.VMEM((2 * ff, width), bf16),
            pltpu.VMEM((8, tokens, 2 * ff), bf16),
            pltpu.VMEM((2, 8, tokens, 2 * ff), bf16),
            pltpu.VMEM((2, 8, tokens, 2 * ff), bf16),
            pltpu.VMEM((4,) + block, bf16),
            pltpu.VMEM((4,) + block, bf16),
            pltpu.VMEM((4,) + block, bf16),
            pltpu.VMEM((4,) + block, bf16),
            pltpu.VMEM((4,) + block, f32),
            dma((3, 4, 1)),
            dma((8, 1)),
            dma((3, 4, 1)),
            dma((8, 1)),
            dma((3, 4, 2)),
            dma((8, 2)),
            dma((12,)),
            dma((12,)),
            dma((2, 2)),
            dma((2, 2)),
            dma((3, 2)),
            dma((3, 2)),
            dma((2, 8)),
            dma((2, 8)),
            dma((4, 2)),
            dma((4, 2)),
            dma((4, 2)),
            dma((4, 2)),
            dma((4,)),
        ],
        compiler_params=pltpu.CompilerParams(
            collective_id=0, has_side_effects=True, vmem_limit_bytes=56 * 2**20
        ),
    )(
        queries[0],
        keys[0],
        values[0],
        segments,
        resid[0],
        output_weight,
        norm_gain[None],
        routes[0].T,
        route_weights[0].T,
        w_gu[0],
        w_down[0],
    )
    return out[None]


def solution(mesh):
    placed = (
        P(("groups", "expert"), "tm", "head"),
        P(("groups", "expert"), "tm", "head"),
        P(("groups", "expert"), "tm", "head"),
        P(("groups", "expert"), None),
        P(("groups", "expert"), "tm", "head"),
        P("head", "expert"),
        P("head"),
        P(("groups", "expert"), "tm", None),
        P(("groups", "expert"), "tm", None),
        P(("tm", "expert"), "head", None),
        P(("tm", "expert"), None, "head"),
    )
    sizes = mesh.shape
    few = (sizes["tm"], sizes["expert"], sizes["head"]) == (8, 2, 2)
    return jax.shard_map(
        fused if few else local,
        mesh=mesh,
        in_specs=placed,
        out_specs=P(("groups", "expert"), "tm", "head"),
        check_vma=False,
    )
```

```python
import math

import jax
import jax.numpy as jnp
from jax import lax
from jax.experimental import pallas as pl
from jax.experimental.pallas import tpu as pltpu
from jax.sharding import PartitionSpec as P

masked_score = -1e30
epsilon = 1e-06
MESH = pl.DeviceIdType.MESH


def deliver(buffer):
    return lax.all_to_all(buffer, ("tm", "expert"), split_axis=0, concat_axis=0, tiled=True)


def local(
    queries,
    keys,
    values,
    segments,
    resid,
    output_weight,
    norm_gain,
    routes,
    route_weights,
    w_gu,
    w_down,
):
    head_size = keys.shape[2]
    tokens = queries.shape[1]
    groups = queries.shape[2] // head_size
    query_blk = queries[0].reshape(tokens, groups, head_size)
    seq_ids = segments[0]
    query_ids = lax.dynamic_slice_in_dim(seq_ids, lax.axis_index("tm") * tokens, tokens)
    score_scale = 1.0 / math.sqrt(head_size)
    running = jnp.full((groups, tokens), masked_score, jnp.float32)
    key_blk = lax.all_gather(keys, "tm", axis=1, tiled=True)[0]
    value_blk = lax.all_gather(values, "tm", axis=1, tiled=True)[0]
    scores = (
        jnp.einsum("tgd,nd->gtn", query_blk, key_blk, preferred_element_type=jnp.float32)
        * score_scale
    )
    allowed = seq_ids[None, None, :] <= query_ids[None, :, None]
    scores = jnp.where(allowed, scores, masked_score)
    newmax = jnp.maximum(running, jnp.max(scores, axis=-1))
    exp_scores = jnp.where(allowed, jnp.exp(scores - newmax[..., None]), 0.0)
    total = jnp.sum(exp_scores, axis=-1)
    weighted = jnp.einsum(
        "gtn,nd->gtd",
        exp_scores.astype(jnp.bfloat16),
        value_blk,
        preferred_element_type=jnp.float32,
    )
    running, total, weighted = (newmax, total, weighted)
    attended = (
        (weighted / total[..., None])
        .transpose(1, 0, 2)
        .reshape(tokens, groups * head_size)
        .astype(jnp.bfloat16)
    )
    partial_value = jnp.dot(
        attended,
        lax.all_gather(output_weight, "expert", axis=1, tiled=True),
        preferred_element_type=jnp.float32,
    )
    width = resid.shape[2]
    full_width = partial_value.shape[1]
    offset = lax.axis_index("head") * width
    placed = lax.dynamic_update_slice_in_dim(
        jnp.zeros((tokens, full_width), jnp.float32), resid[0].astype(jnp.float32), offset, 1
    )
    hidden_in = lax.psum((partial_value + placed).astype(jnp.bfloat16), "head").astype(jnp.float32)
    inv_rms = lax.rsqrt(jnp.mean(hidden_in * hidden_in, axis=-1) + epsilon)
    hidden_half = lax.dynamic_slice_in_dim(hidden_in, offset, width, 1)
    normed_half = (hidden_half * inv_rms[:, None] * norm_gain).astype(jnp.bfloat16)
    expert_total = lax.axis_size("tm") * lax.axis_size("expert")
    top_count = routes.shape[2]
    capacity = min(tokens, 3 * tokens * top_count // (2 * expert_total))
    flat_routes = routes[0].reshape(-1)
    flat_weights = route_weights[0].reshape(-1)
    onehot = (flat_routes[:, None] == jnp.arange(expert_total, dtype=jnp.int32)[None, :]).astype(
        jnp.int32
    )
    earlier = jnp.cumsum(onehot, axis=0) - onehot
    rank = jnp.sum(earlier * onehot, axis=1)
    slot_ids = flat_routes * capacity + rank
    slot_range = jnp.arange(expert_total * capacity, dtype=jnp.int32)
    pair_match = slot_range[:, None] == slot_ids[None, :]
    dispatch = jnp.sum(
        pair_match.reshape(expert_total * capacity, tokens, top_count).astype(jnp.float32), axis=2
    )
    send_rows = jnp.dot(
        dispatch.astype(jnp.bfloat16), normed_half, preferred_element_type=jnp.float32
    ).astype(jnp.bfloat16)
    arrived = deliver(send_rows.reshape(expert_total, capacity, width))
    arrived_rows = arrived.reshape(expert_total * capacity, width)
    block_gate = jnp.dot(arrived_rows, w_gu[0], preferred_element_type=jnp.float32).astype(
        jnp.bfloat16
    )
    gate_up = lax.psum(block_gate, "head").astype(jnp.float32)
    feedforward_count = w_down.shape[1]
    activated = (
        jax.nn.silu(gate_up[:, :feedforward_count]) * gate_up[:, feedforward_count:]
    ).astype(jnp.bfloat16)
    expert_out = jnp.dot(activated, w_down[0], preferred_element_type=jnp.float32).astype(
        jnp.bfloat16
    )
    returned = deliver(expert_out.reshape(expert_total, capacity, width))
    returned_rows = returned.reshape(expert_total * capacity, width).astype(jnp.float32)
    combine = jnp.sum(
        (pair_match.astype(jnp.float32) * flat_weights[None, :]).reshape(
            expert_total * capacity, tokens, top_count
        ),
        axis=2,
    )
    mixed = jnp.dot(combine.T, returned_rows, precision=lax.Precision.HIGHEST)
    layer_out = (hidden_half + mixed).astype(jnp.bfloat16)
    return layer_out[None]


def fused_kernel(
    q_ref,
    k_ref,
    v_ref,
    seg_ref,
    resid_hbm,
    ow_hbm,
    gain_ref,
    routes_ref,
    rw_ref,
    wgu_hbm,
    wdn_hbm,
    out_ref,
    kv,
    coef,
    attended,
    core_send,
    core_recv,
    diag_send,
    diag_recv,
    projected,
    squares,
    hidden,
    rows,
    resid_ref,
    ow_ref,
    gu_own,
    gu_other,
    down,
    acts,
    part_send,
    part_recv,
    y_send,
    y_recv,
    z_send,
    z_recv,
    kept,
    kv_ss,
    kv_rs,
    coef_ss,
    coef_rs,
    row_ss,
    row_rs,
    w_ss,
    w_rs,
    att_ss,
    att_rs,
    mid_ss,
    mid_rs,
    part_ss,
    part_rs,
    y_ss,
    y_rs,
    z_ss,
    z_rs,
    load_sems,
):
    f32, bf16 = jnp.float32, jnp.bfloat16
    tm = lax.axis_index("tm")
    x = lax.axis_index("expert")
    h = lax.axis_index("head")
    z, y = tm // 2, tm % 2
    first = z - 1 + 2 * ((3 - z) // 3)
    last = 3 * (1 - z // 2)
    line = [first, 6 - z - first - last, last]
    to_y = {"tm": z * 2 + 1 - y}
    to_z = [{"tm": u * 2 + y} for u in line]
    to_up, to_down = {"tm": tm + 2}, {"tm": tm - 2}
    to_x = {"expert": 1 - x}
    to_core = {"head": 1 - h}
    to_diag = {"expert": 1 - x, "head": 1 - h}
    tokens = q_ref.shape[0]
    hd = k_ref.shape[1]
    heads = q_ref.shape[1] // hd
    width = resid_ref.shape[1]
    ff = wdn_hbm.shape[0]
    loads = [
        pltpu.make_async_copy(src, dst, load_sems.at[i])
        for i, (src, dst) in enumerate(
            [
                (ow_hbm, ow_ref),
                (resid_hbm, resid_ref),
                (wgu_hbm, gu_own),
                (wdn_hbm, down.at[pl.ds(0, ff)]),
            ]
        )
    ]
    for load in loads:
        load.start()
    experts = coef.shape[0] // 8

    def remote(src, dst, ss, rs, dev):
        return pltpu.make_async_remote_copy(
            src_ref=src, dst_ref=dst, send_sem=ss, recv_sem=rs, device_id=dev, device_id_type=MESH
        )

    class Spread:
        def __init__(self, at, chunks, ss, rs):
            self.at, self.chunks, self.ss, self.rs = at, chunks, ss, rs

        def copies(self, u, c):
            slot = 2 * u + y
            here = self.at(slot, c)
            rs = self.rs.at[slot, c]
            return [
                remote(here, here, self.ss.at[way, u, c], rs, dev)
                for way, dev in enumerate((to_up, to_down, to_y))
            ]

        def send(self, u, c):
            up, down, across = self.copies(u, c)
            pl.when((z < 3) & (u <= z))(up.start)
            pl.when((z > 0) & (u >= z))(down.start)
            across.start()

        def arrive(self, slot, c):
            here = self.at(slot, c)
            remote(here, here, self.ss.at[2, 0, c], self.rs.at[slot, c], to_y).wait_recv()

        def begin(self):
            for c in range(self.chunks):
                self.send(z, c)

        def relay(self, u, c):
            self.arrive(2 * u + y, c)
            self.send(u, c)

        def finish(self):
            for u in range(4):
                for c in range(self.chunks):
                    up, down, across = self.copies(u, c)
                    pl.when((z < 3) & (u <= z))(up.wait_send)
                    pl.when((z > 0) & (u >= z))(down.wait_send)
                    across.wait_send()

    class Direct(Spread):
        def copies(self, u, c):
            here = self.at(2 * u + y, c)
            return remote(here, here, self.ss.at[2, u, c], self.rs.at[2 * u + y, c], to_y)

        def sends(self):
            here, rs = self.at(tm, 0), self.rs.at[tm, 0]
            return [remote(here, here, self.ss.at[0, i, 0], rs, to_z[i]) for i in range(3)]

        def begin(self):
            self.copies(z, 0).start()
            for copy in self.sends():
                copy.start()

        def send(self, u, c):
            self.copies(u, c).start()

        def finish(self):
            for u in range(4):
                self.copies(u, 0).wait_send()
            for copy in self.sends():
                copy.wait_send()

    barrier = pltpu.get_barrier_semaphore()
    peers = [to_y, to_x, to_core, to_diag] + to_z
    for dev in peers:
        pl.semaphore_signal(barrier, inc=1, device_id=dev, device_id_type=MESH)

    kv[tm, 0] = k_ref[...]
    kv[tm, 1] = v_ref[...]
    lanes = lax.broadcasted_iota(jnp.int32, (tokens, 128), 1)
    numbers = lax.broadcasted_iota(jnp.int32, (experts, tokens), 0)
    dense = jnp.zeros((experts, tokens), f32)
    for k in range(routes_ref.shape[0]):
        dense += jnp.where(numbers == routes_ref[k : k + 1, :], rw_ref[k : k + 1, :], 0.0)
    coef[pl.ds(tm * experts, experts), :] = dense

    pl.semaphore_wait(barrier, len(peers))

    kv_spread = Direct(lambda s, c: kv.at[s], 1, kv_ss, kv_rs)
    coef_spread = Direct(lambda s, c: coef.at[pl.ds(s * experts, experts)], 1, coef_ss, coef_rs)
    piece = tokens // row_rs.shape[1]
    row_spread = Spread(
        lambda s, c: rows.at[s, pl.ds(c * piece, piece)], row_rs.shape[1], row_ss, row_rs
    )
    kv_spread.begin()
    gu_rows = wgu_hbm.shape[0] // 8
    parts = 2
    part = width // parts
    dn_rows = ff // 2
    w_parts = [
        (wgu_hbm.at[pl.ds(i * gu_rows, gu_rows)], gu_other.at[pl.ds(i * gu_rows, gu_rows)])
        for i in range(8)
    ] + [
        (
            wdn_hbm.at[pl.ds(r * dn_rows, dn_rows), pl.ds(c * part, part)],
            down.at[pl.ds(ff + r * dn_rows, dn_rows), pl.ds(c * part, part)],
        )
        for c in range(parts)
        for r in range(2)
    ]
    w_copies = [
        remote(src, dst, w_ss.at[i], w_rs.at[i], to_x) for i, (src, dst) in enumerate(w_parts)
    ]
    waiting = list(w_copies)

    def some_weights(count):
        for copy in waiting[:count]:
            copy.start()
        del waiting[:count]

    some_weights(3)
    coef_spread.begin()
    for u in line:
        kv_spread.relay(u, 0)
    for u in line:
        coef_spread.relay(u, 0)
    kv_spread.arrive(tm + 1 - 2 * y, 0)
    for u in line:
        kv_spread.arrive(2 * u + 1 - y, 0)

    own_ids = seg_ref[:, pl.ds(pl.multiple_of(tm * tokens, tokens), tokens)].astype(f32)
    own_column = jnp.broadcast_to(own_ids, (tokens, tokens)).T
    all_ids = jnp.broadcast_to(seg_ref[...].astype(f32), (tokens, 8 * tokens))
    allowed = all_ids <= jnp.concatenate([own_column] * 8, axis=1)
    key_all = kv[:, 0].reshape(8 * tokens, hd)
    value_all = kv[:, 1].reshape(8 * tokens, hd)
    scale = 1.0 / math.sqrt(hd)
    pieces = row_spread.chunks
    att_copies = {}
    for c in range(pieces):
        some = pl.ds(c * piece, piece)
        allowed_here = allowed[c * piece : (c + 1) * piece]
        for g in range(heads):
            cols = pl.ds(g * hd, hd)
            scores = lax.dot_general(
                q_ref[some, cols], key_all, (((1,), (1,)), ((), ())), preferred_element_type=f32
            )
            scores = jnp.where(allowed_here, scores * scale, masked_score)
            top = jnp.max(scores, axis=1, keepdims=True)
            probs = jnp.exp(scores - top)
            total = jnp.sum(probs, axis=1, keepdims=True)
            summed = jnp.dot(probs.astype(bf16), value_all, preferred_element_type=f32)
            attended[x, some, cols] = (summed / total).astype(bf16)
            if g % 4 == 3:
                here = attended.at[x, some, pl.ds((g - 3) * hd, 4 * hd)]
                i = c, g // 4
                att_copies[i] = remote(here, here, att_ss.at[i], att_rs.at[i], to_x)
                att_copies[i].start()

    def mid(c, i, src, dst, dev):
        some = pl.ds(c * piece, piece)
        return remote(src.at[some], dst.at[some], mid_ss.at[i, c], mid_rs.at[i, c], dev)

    core_copies = [mid(c, 0, core_send, core_recv, to_core) for c in range(pieces)]
    diag_copies = [mid(c, 1, diag_send, diag_recv, to_diag) for c in range(pieces)]
    sq_copies = [mid(c, 2, squares.at[0], squares.at[1], to_core) for c in range(pieces)]
    loads[0].wait()
    for c in range(pieces):
        some = pl.ds(c * piece, piece)
        for i in range(2):
            att_copies[c, i].wait()
        core_send[some] = jnp.dot(
            attended[1 - h, some], ow_ref[...], preferred_element_type=f32
        ).astype(bf16)
        core_copies[c].start()
        projected[some] = jnp.dot(attended[h, some], ow_ref[...], preferred_element_type=f32)
    some_weights(0)
    for c in range(pieces):
        some = pl.ds(c * piece, piece)
        core_copies[c].wait()
        projected[some] += core_recv[some].astype(f32)
        diag_send[some] = projected[some].astype(bf16)
        pl.when(x != h)(diag_copies[c].start)
    some_weights(6)
    loads[1].wait()
    for c in range(pieces):
        some = pl.ds(c * piece, piece)

        @pl.when(x != h)
        def _():
            diag_copies[c].wait()
            projected[some] = diag_recv[some].astype(f32)

        full = projected[some] + resid_ref[some].astype(f32)
        hidden[some] = full
        own_sum = jnp.sum(full * full, axis=1, keepdims=True)
        squares[0, some] = jnp.broadcast_to(own_sum, (piece, 128))
        sq_copies[c].start()
    for c in range(pieces):
        some = pl.ds(c * piece, piece)
        sq_copies[c].wait()
        mean = (squares[0, some][:, 0:1] + squares[1, some][:, 0:1]) * (1.0 / (2 * width))
        rows[tm, some] = (hidden[some] * lax.rsqrt(mean + epsilon) * gain_ref[...]).astype(bf16)
        row_spread.send(z, c)
    coef_spread.arrive(tm + 1 - 2 * y, 0)
    for u in line:
        coef_spread.arrive(2 * u + 1 - y, 0)
    by_token = coef[...].T

    def part_copy(s, which):
        return remote(
            part_send.at[which, s],
            part_recv.at[which, s],
            part_ss.at[which, s],
            part_rs.at[which, s],
            to_core,
        )

    def gate_up(s, which, weights):
        part_send[which, s] = jnp.dot(
            rows[s], weights[...], preferred_element_type=f32
        ).astype(bf16)
        part_copy(s, which).start()

    loads[2].wait()
    gate_up(tm, 0, gu_own)

    def across(u):
        for c in range(row_spread.chunks):
            row_spread.arrive(2 * u + 1 - y, c)
        gate_up(2 * u + 1 - y, 0, gu_own)

    for i, u in enumerate(line):
        for c in range(row_spread.chunks):
            row_spread.relay(u, c)
            some_weights(1)
        gate_up(2 * u + y, 0, gu_own)
        across(z if i == 0 else line[i - 1])
    some_weights(12)

    mine = [tm * 2 + x, tm * 2 + 1 - x]

    def activate(s):
        for which in range(2):
            part_copy(s, which).wait_recv()
            both = part_send[which, s].astype(f32) + part_recv[which, s].astype(f32)
            gate, up = both[:, :ff], both[:, ff:]
            wanted = jnp.where(lanes == s * experts + mine[which], by_token, 0.0)
            weight = jnp.sum(wanted, axis=1, keepdims=True)
            acts[s, :, which * ff : (which + 1) * ff] = (
                gate / (1.0 + jnp.exp(-gate)) * up * weight
            ).astype(bf16)

    for copy in w_copies[:8]:
        copy.wait_recv()
    near, middle, distant = line
    late = 2 * distant + 1 - y
    early = [2 * u + 1 - y for u in (middle, near, z)] + [
        2 * u + y for u in (middle, near, distant, z)
    ]
    for s in early:
        gate_up(s, 1, gu_other)
    for s in early[:2]:
        activate(s)

    def y_copy(u, c):
        cols = pl.ds(c * part, part)
        return remote(y_send.at[u, :, cols], y_recv.at[u, :, cols], y_ss.at[u, c], y_rs.at[u, c], to_y)

    def z_copy(u, c, mine):
        cols = pl.ds(c * part, part)
        slot = z if mine else u
        return remote(
            z_send.at[u, :, cols],
            z_recv.at[slot, :, cols],
            z_ss.at[u, c],
            z_rs.at[slot, c],
            {"tm": u * 2 + y},
        )

    def pass_on(u, c):
        cols = pl.ds(c * part, part)
        y_copy(u, c).wait_recv()
        z_send[u, :, cols] = (kept[u, :, cols] + y_recv[u, :, cols].astype(f32)).astype(bf16)
        z_copy(u, c, True).start()

    def down_dot(s, cols):
        return jnp.dot(acts[s], down[:, cols], preferred_element_type=f32)

    def give(u, c):
        cols = pl.ds(c * part, part)
        y_send[u, :, cols] = down_dot(2 * u + 1 - y, cols).astype(bf16)
        y_copy(u, c).start()

    def keep(u, c):
        cols = pl.ds(c * part, part)
        kept[u, :, cols] = down_dot(2 * u + y, cols)

    loads[3].wait()
    for copy in w_copies[8:10]:
        copy.wait_recv()
    give(middle, 0)
    give(near, 0)
    for s in early[2:]:
        activate(s)
    across(distant)
    gate_up(late, 1, gu_other)
    activate(late)
    give(distant, 0)
    give(z, 0)
    for u in (middle, near, distant, z):
        keep(u, 0)
    pass_on(middle, 0)
    for copy in w_copies[10:12]:
        copy.wait_recv()
    for u in (distant, middle, near, z):
        give(u, 1)
    pass_on(near, 0)
    for u in (distant, middle, near, z):
        keep(u, 1)
    pass_on(distant, 0)
    for u in (distant, middle, near):
        pass_on(u, 1)
    for c in range(parts):
        cols = pl.ds(c * part, part)
        y_copy(z, c).wait_recv()
        mixed = hidden[:, cols] + kept[z, :, cols] + y_recv[z, :, cols].astype(f32)
        for u in line:
            z_copy(u, c, False).wait_recv()
            mixed += z_recv[u, :, cols].astype(f32)
        out_ref[:, cols] = mixed.astype(bf16)

    for spread in (kv_spread, coef_spread, row_spread):
        spread.finish()
    for copy in w_copies:
        copy.wait_send()
    for s in range(8):
        for which in range(2):
            part_copy(s, which).wait_send()
    for u in range(4):
        for c in range(parts):
            y_copy(u, c).wait_send()
    for u in line:
        for c in range(parts):
            z_copy(u, c, True).wait_send()


def fused(
    queries,
    keys,
    values,
    segments,
    resid,
    output_weight,
    norm_gain,
    routes,
    route_weights,
    w_gu,
    w_down,
):
    bf16, f32 = jnp.bfloat16, jnp.float32
    tokens, width = resid.shape[1:]
    hd = keys.shape[2]
    ff = w_down.shape[1]
    experts = lax.axis_size("tm") * lax.axis_size("expert")
    block = (tokens, width)
    dma = pltpu.SemaphoreType.DMA
    out = pl.pallas_call(
        fused_kernel,
        out_shape=jax.ShapeDtypeStruct(block, bf16),
        in_specs=[
            pl.BlockSpec(memory_space=pl.ANY if i in (4, 5, 9, 10) else pltpu.VMEM)
            for i in range(11)
        ],
        out_specs=pl.BlockSpec(memory_space=pltpu.VMEM),
        scratch_shapes=[
            pltpu.VMEM((8, 2, tokens, hd), bf16),
            pltpu.VMEM((8 * experts, tokens), f32),
            pltpu.VMEM((2, tokens, queries.shape[2]), bf16),
            pltpu.VMEM((tokens, output_weight.shape[1]), bf16),
            pltpu.VMEM((tokens, output_weight.shape[1]), bf16),
            pltpu.VMEM(block, bf16),
            pltpu.VMEM(block, bf16),
            pltpu.VMEM(block, f32),
            pltpu.VMEM((2, tokens, 128), f32),
            pltpu.VMEM(block, f32),
            pltpu.VMEM((8,) + block, bf16),
            pltpu.VMEM(block, bf16),
            pltpu.VMEM(output_weight.shape, bf16),
            pltpu.VMEM(w_gu.shape[1:], bf16),
            pltpu.VMEM(w_gu.shape[1:], bf16),
            pltpu.VMEM((2 * ff, width), bf16),
            pltpu.VMEM((8, tokens, 2 * ff), bf16),
            pltpu.VMEM((2, 8, tokens, 2 * ff), bf16),
            pltpu.VMEM((2, 8, tokens, 2 * ff), bf16),
            pltpu.VMEM((4,) + block, bf16),
            pltpu.VMEM((4,) + block, bf16),
            pltpu.VMEM((4,) + block, bf16),
            pltpu.VMEM((4,) + block, bf16),
            pltpu.VMEM((4,) + block, f32),
            dma((3, 4, 1)),
            dma((8, 1)),
            dma((3, 4, 1)),
            dma((8, 1)),
            dma((3, 4, 2)),
            dma((8, 2)),
            dma((12,)),
            dma((12,)),
            dma((2, 2)),
            dma((2, 2)),
            dma((3, 2)),
            dma((3, 2)),
            dma((2, 8)),
            dma((2, 8)),
            dma((4, 2)),
            dma((4, 2)),
            dma((4, 2)),
            dma((4, 2)),
            dma((4,)),
        ],
        compiler_params=pltpu.CompilerParams(
            collective_id=0, has_side_effects=True, vmem_limit_bytes=56 * 2**20
        ),
    )(
        queries[0],
        keys[0],
        values[0],
        segments,
        resid[0],
        output_weight,
        norm_gain[None],
        routes[0].T,
        route_weights[0].T,
        w_gu[0],
        w_down[0],
    )
    return out[None]


def solution(mesh):
    placed = (
        P(("groups", "expert"), "tm", "head"),
        P(("groups", "expert"), "tm", "head"),
        P(("groups", "expert"), "tm", "head"),
        P(("groups", "expert"), None),
        P(("groups", "expert"), "tm", "head"),
        P("head", "expert"),
        P("head"),
        P(("groups", "expert"), "tm", None),
        P(("groups", "expert"), "tm", None),
        P(("tm", "expert"), "head", None),
        P(("tm", "expert"), None, "head"),
    )
    sizes = mesh.shape
    few = (sizes["tm"], sizes["expert"], sizes["head"]) == (8, 2, 2)
    return jax.shard_map(
        fused if few else local,
        mesh=mesh,
        in_specs=placed,
        out_specs=P(("groups", "expert"), "tm", "head"),
        check_vma=False,
    )
```
